32 devices in a mesh: dp: 8 (over z, x), row: 2 (over y), col: 2 (over core).
Axes of the slice: x: 2, y: 2, z: 4, core: 2. Of those that a mesh axis runs over, the one named last changes fastest.
Arguments:
- tokens: bfloat16 [32768, 640], P('dp', ('row', 'col')), may hold values from -6 to 6
- w_query: bfloat16 [640, 1024], P('row', 'col'), may hold values from -0.25 to 0.25
- w_key: bfloat16 [640, 256], P('row', 'col'), may hold values from -0.25 to 0.25
- w_value: bfloat16 [640, 256], P('row', 'col'), may hold values from -0.25 to 0.25
- w_out: bfloat16 [1024, 640], P('col', 'row'), may hold values from -0.1875 to 0.1875
- w_gate: bfloat16 [640, 2048], P('row', 'col'), may hold values from -0.25 to 0.25
- w_up: bfloat16 [640, 2048], P('row', 'col'), may hold values from -0.25 to 0.25
- w_down: bfloat16 [2048, 640], P('col', 'row'), may hold values from -0.125 to 0.125
- gain_input: float32 [640], P(('row', 'col')), may hold values from 0.1 to 1.9
- gain_post_attn: float32 [640], P(('row', 'col')), may hold values from 0.1 to 1.9
- gain_pre_ffn: float32 [640], P(('row', 'col')), may hold values from 0.1 to 1.9
- gain_post_ffn: float32 [640], P(('row', 'col')), may hold values from 0.1 to 1.9
- gain_query: float32 [256], replicated, may hold values from 0.1 to 1.9
- gain_key: float32 [256], replicated, may hold values from 0.1 to 1.9
- segment_ids: int32 [32768], P('dp'), may hold values from 0 to 127, never falling along the last dimension, each value on 1 to 512 neighbouring positions
- positions: int32 [32768], P('dp'), may hold values from 0 to 8191
- cotangent: bfloat16 [32768, 640], P('dp', ('row', 'col')), may hold values from -6 to 6
Outputs:
- output: bfloat16 [32768, 640], P('dp', ('row', 'col'))
- grad_tokens: bfloat16 [32768, 640], P('dp', ('row', 'col'))
- grad_w_query: float32 [640, 1024], P('row', 'col')
- grad_w_key: float32 [640, 256], P('row', 'col')
- grad_w_value: float32 [640, 256], P('row', 'col')
- grad_w_out: float32 [1024, 640], P('col', 'row')
- grad_w_gate: float32 [640, 2048], P('row', 'col')
- grad_w_up: float32 [640, 2048], P('row', 'col')
- grad_w_down: float32 [2048, 640], P('col', 'row')
- grad_gain_input: float32 [640], P(('row', 'col'))
- grad_gain_post_attn: float32 [640], P(('row', 'col'))
- grad_gain_pre_ffn: float32 [640], P(('row', 'col'))
- grad_gain_post_ffn: float32 [640], P(('row', 'col'))
- grad_gain_query: float32 [256], replicated
- grad_gain_key: float32 [256], replicated
The draws below stay inside these ranges and needn't reach their ends.
Inputs may be any that keep to these rules, and one draw needn't show every extreme that they name: segment_ids never fall from one token to the next; each document has 1 to min(512, 1024) tokens.
All inputs are finite; a program needn't handle non-finite values.
Results may differ from the reference program's by a relative error of at most 0.02.
Values may be sent and summed in bfloat16 or wider, within the bound.
A program may use at most 192 MiB of HBM per device.

```python
import math
import jax
import jax.numpy as jnp
import numpy as np
from jax import lax

D = 640
HEADS = 4
HD = 256
FF = 2048
LEN = 1024
TOKENS = 32768


def set_ends(array, own_key, low, largest):
    longest = array.shape.index(max(array.shape))
    spots = []
    for shift in (0, 1):
        where = [jax.random.randint(jax.random.fold_in(own_key, axis), (), 0, length) for axis, length in enumerate(array.shape)]
        where[longest] = (where[longest] + shift) % array.shape[longest]
        spots.append(tuple(where))
    return array.at[spots[0]].set(low).at[spots[1]].set(largest)


def level_of(rng, shape, split, least, high):
    def one(position, parts):
        steps = jax.random.uniform(jax.random.fold_in(jax.random.fold_in(rng, 6), position), (parts,), jnp.float32, least / len(split), high / len(split))
        return jnp.repeat(jnp.exp(steps), shape[position] // parts).reshape((-1,) + (1,) * (len(shape) - position - 1))

    level = one(*split[0])
    for cut in split[1:]:
        level = level * one(*cut)
    return level


def split_up(count, total, reach, lean):
    portions = [(1 << 20) // math.isqrt(standing ** lean) + 1 for standing in range(2, count + 1)]
    spare, given = total - reach - (count - 1), [1] * (count - 1)
    while spare > 0:
        movable = [i for i in range(count - 1) if given[i] < reach]
        pool, left = sum([portions[i] for i in movable]), spare
        for i in movable:
            more = min(reach - given[i], max(1, left * portions[i] // pool), spare)
            given[i] = given[i] + more
            spare = spare - more
    return np.array([reach] + given)


def ragged_sizes(key, count, total, bound, lean):
    if count == 2:
        one = jax.random.randint(key, (), max(1, total - bound), min(bound, total - 1) + 1)
        return jnp.stack([one, total - one])
    tallies = jnp.asarray(split_up(count, total, bound, lean), jnp.int32)
    pairs = (count - 1) // 2
    donor, taker = tallies[1:1 + 2 * pairs:2], tallies[2:2 + 2 * pairs:2]
    slack = jnp.minimum(donor - 1, bound - taker)
    passed = jax.random.randint(jax.random.fold_in(key, 1), (pairs,), 0, 1 << 20) % (slack + 1)
    tallies = tallies.at[1:1 + 2 * pairs:2].set(donor - passed).at[2:2 + 2 * pairs:2].set(taker + passed)
    return tallies[jax.random.permutation(jax.random.fold_in(key, 2), count)]


def bell_draw(stream_key, shape, spread, limit, cuts=(), kind=jnp.bfloat16):
    entries = jax.random.normal(stream_key, shape, jnp.float32) * spread
    if len(cuts) > 0:
        entries = level_of(stream_key, shape, cuts, -0.22, 0.18) * entries
    return jnp.clip(entries, min=-limit, max=limit).astype(kind)


def setup_inputs(seed: int = 0) -> dict:
    key_list = jax.random.split(jax.random.key(seed), 18)
    tokens = bell_draw(key_list[0], (TOKENS, D), 1.0, 6.0, ((0, 8), (1, 4)))
    w_query = bell_draw(key_list[1], (D, HEADS * HD), D ** -0.5, 0.25, ((0, 2), (1, 2)))
    w_key = bell_draw(key_list[2], (D, HD), D ** -0.5, 0.25, ((0, 2), (1, 2)))
    w_value = bell_draw(key_list[3], (D, HD), D ** -0.5, 0.25, ((0, 2), (1, 2)))
    w_out = bell_draw(key_list[4], (HEADS * HD, D), (HEADS * HD) ** -0.5, 0.1875, ((0, 2), (1, 2)))
    w_gate = bell_draw(key_list[5], (D, FF), D ** -0.5, 0.25, ((0, 2), (1, 2)))
    w_up = bell_draw(key_list[6], (D, FF), D ** -0.5, 0.25, ((0, 2), (1, 2)))
    w_down = bell_draw(key_list[7], (FF, D), FF ** -0.5, 0.125, ((0, 2), (1, 2)))
    gain_input = jnp.clip(1.0 + 0.18 * jax.random.normal(key_list[8], (D,), jnp.float32), 0.1, 1.9)
    gain_post_attn = jnp.clip(1.0 + 0.18 * jax.random.normal(key_list[9], (D,), jnp.float32), 0.1, 1.9)
    gain_pre_ffn = jnp.clip(1.0 + 0.18 * jax.random.normal(key_list[10], (D,), jnp.float32), 0.1, 1.9)
    gain_post_ffn = jnp.clip(1.0 + 0.18 * jax.random.normal(key_list[11], (D,), jnp.float32), 0.1, 1.9)
    gain_query = jnp.clip(1.0 + 0.18 * jax.random.normal(key_list[12], (HD,), jnp.float32), 0.1, 1.9)
    gain_key = jnp.clip(1.0 + 0.18 * jax.random.normal(key_list[13], (HD,), jnp.float32), 0.1, 1.9)
    segment_ids = jnp.searchsorted(jnp.cumsum(ragged_sizes(key_list[14], 2 * TOKENS // min(512, LEN), TOKENS, min(512, LEN), 1)), jnp.arange(TOKENS), side="right").astype(jnp.int32)
    positions = set_ends(jax.random.randint(key_list[15], (TOKENS,), 0, 8192), jax.random.fold_in(key_list[15], 1), 0, 8191).astype(jnp.int32)
    cotangent = bell_draw(key_list[16], (TOKENS, D), 1.0, 6.0, ((0, 8), (1, 4)))
    return {"tokens": tokens, "w_query": w_query, "w_key": w_key, "w_value": w_value, "w_out": w_out, "w_gate": w_gate, "w_up": w_up, "w_down": w_down, "gain_input": gain_input, "gain_post_attn": gain_post_attn, "gain_pre_ffn": gain_pre_ffn, "gain_post_ffn": gain_post_ffn, "gain_query": gain_query, "gain_key": gain_key, "segment_ids": segment_ids, "positions": positions, "cotangent": cotangent}


EPSILON = 1e-06
ROPE_BASE = 1000000.0
MASK_VALUE = -1000000000.0

@jax.custom_vjp
def low(v):
    return lax.optimization_barrier(v.astype(jnp.bfloat16)).astype(jnp.float32)

@jax.custom_vjp
def low_back(v):
    return v

def low_keep(v):
    return (low(v), None)

def low_pass(kept, grad):
    return (grad,)

def back_keep(v):
    return (v, None)

def back_low(kept, grad):
    return (low(grad),)
low.defvjp(low_keep, low_pass)
low_back.defvjp(back_keep, back_low)

def rms(values, gain_vec):
    inv_rms = lax.rsqrt(lax.optimization_barrier(jnp.mean(values * values, axis=-1, keepdims=True)) + EPSILON)
    return values * inv_rms * gain_vec

def rotary_tables(positions, width):
    half_width = width // 2
    frequency = jnp.exp(jnp.arange(half_width, dtype=jnp.float32) * (-2.0 * math.log(ROPE_BASE) / width))
    angles = positions.astype(jnp.float32)[:, None] * frequency[None, :]
    return (jnp.cos(angles), jnp.sin(angles))

def head_prep(values, gain_vec, cosine, sine):
    normed = rms(values, gain_vec)
    half_width = normed.shape[-1] // 2
    first_half = normed[..., :half_width]
    second = normed[..., half_width:]
    return jnp.concatenate([first_half * cosine - second * sine, second * cosine + first_half * sine], axis=-1)

def reference(tokens, w_query, w_key, w_value, w_out, w_gate, w_up, w_down, gain_input, gain_post_attn, gain_pre_ffn, gain_post_ffn, gain_query, gain_key, segment_ids, positions, cotangent):
    highest = lax.Precision.HIGHEST
    seq_count = TOKENS // LEN
    cosine, sine = rotary_tables(positions, HD)
    causal = jnp.arange(LEN)[:, None] >= jnp.arange(LEN)[None, :]
    seg_blocks = segment_ids.reshape(seq_count, LEN)

    def attend(inputs):
        query_seq, key_seq, value_seq, seg_seq = inputs
        allowed = causal & (seg_seq[:, None] == seg_seq[None, :])
        scale_factor = query_seq.shape[-1] ** (-0.5)
        scores = low_back(jnp.einsum('qhd,kd->hqk', query_seq, key_seq, precision=highest) * scale_factor)
        scores = jnp.where(allowed[None, :, :], scores, MASK_VALUE)
        row_max = lax.optimization_barrier(jnp.max(scores, axis=2, keepdims=True))
        exp_scores = jnp.exp(scores - row_max)
        soft_weights = low(exp_scores / lax.optimization_barrier(jnp.sum(exp_scores, axis=2, keepdims=True)))
        return jnp.einsum('hqk,kd->qhd', soft_weights, value_seq, precision=highest)

    def forward(block_in, query_w, key_w, value_w, out_w, gate_w, up_w, down_w, input_g, post_attn_g, pre_ffn_g, post_ffn_g, query_g, key_g):
        act_one = low(rms(block_in, input_g))
        query_raw = low_back(jnp.dot(act_one, query_w, precision=highest))
        key_raw = low_back(jnp.dot(act_one, key_w, precision=highest))
        value_act = low(low_back(jnp.dot(act_one, value_w, precision=highest)))
        query_heads = low(head_prep(query_raw.reshape(TOKENS, HEADS, HD), query_g, cosine[:, None, :], sine[:, None, :]))
        key_head = low(head_prep(key_raw, key_g, cosine, sine))
        heads_out = lax.map(jax.checkpoint(attend), (query_heads.reshape(seq_count, LEN, HEADS, HD), key_head.reshape(seq_count, LEN, HD), value_act.reshape(seq_count, LEN, HD), seg_blocks))
        attn = low(low_back(heads_out.reshape(TOKENS, HEADS * HD)))
        branch_attn = low_back(jnp.dot(attn, out_w, precision=highest))
        middle = block_in + rms(branch_attn, post_attn_g)
        act_two = low(rms(middle, pre_ffn_g))
        gate_act = low_back(jnp.dot(act_two, gate_w, precision=highest))
        up_act = low_back(jnp.dot(act_two, up_w, precision=highest))
        hidden = low(jax.nn.gelu(gate_act, approximate=True) * up_act)
        branch_ffn = low_back(jnp.dot(hidden, down_w, precision=highest))
        return middle + rms(branch_ffn, post_ffn_g)
    floats = tuple((item.astype(jnp.float32) for item in (tokens, w_query, w_key, w_value, w_out, w_gate, w_up, w_down, gain_input, gain_post_attn, gain_pre_ffn, gain_post_ffn, gain_query, gain_key)))
    result, pull_back = jax.vjp(forward, *floats)
    grads = pull_back(cotangent.astype(jnp.float32))
    return (result.astype(jnp.bfloat16), grads[0].astype(jnp.bfloat16), grads[1], grads[2], grads[3], grads[4], grads[5], grads[6], grads[7], grads[8], grads[9], grads[10], grads[11], grads[12], grads[13])
```

```python
import math

import jax
import jax.numpy as jnp
from jax import lax
from jax.experimental import pallas as pl
from jax.experimental.pallas import tpu as pltpu
from jax.sharding import PartitionSpec as P

D = 640
HEADS = 4
HD = 256
FF = 2048
LEN = 1024

EPSILON = 1e-06
ROPE_BASE = 1000000.0
MASK_VALUE = -1000000000.0
GROUP = ("row", "col")
BF16 = jnp.bfloat16
F32 = jnp.float32
SCALE = HD ** -0.5


def dot(left, right):
    return jnp.dot(left, right, preferred_element_type=F32)


def dot_rows(left, right):
    return lax.dot_general(left, right, (((0,), (0,)), ((), ())), preferred_element_type=F32)


def dot_cols(left, right):
    return lax.dot_general(left, right, (((1,), (1,)), ((), ())), preferred_element_type=F32)


def inverse_rms(values):
    return lax.rsqrt(jnp.mean(values * values, axis=-1, keepdims=True) + EPSILON)


def norm_back(values, inv_rms, gain, grad):
    weighted = grad * gain
    inner = jnp.mean(weighted * values, axis=-1, keepdims=True)
    return inv_rms * weighted - values * (inv_rms * inv_rms * inv_rms * inner)


def gain_back(values, inv_rms, grad):
    return jnp.sum(grad * values * inv_rms, axis=0)


def rotary_tables(positions):
    half = HD // 2
    frequency = jnp.exp(jnp.arange(half, dtype=F32) * (-2.0 * math.log(ROPE_BASE) / HD))
    angles = positions.astype(F32)[:, None] * frequency[None, :]
    return (jnp.cos(angles), jnp.sin(angles))


def gather_blocks(block):
    rows, cols = lax.axis_size("row"), lax.axis_size("col")
    return lax.all_gather(block, GROUP).reshape(rows, cols, *block.shape)


def scatter_blocks(blocks):
    blocks = blocks.reshape(-1, *blocks.shape[2:])
    return lax.psum_scatter(blocks, GROUP, scatter_dimension=0)


def to_tokens(block):
    return lax.all_to_all(block, GROUP, split_axis=0, concat_axis=1, tiled=True)


def to_features(block):
    return lax.all_to_all(block, GROUP, split_axis=1, concat_axis=0, tiled=True)


BLOCK = 256
REACH = 512


def window(start):
    return max(0, start - REACH), start + BLOCK


def joined(ref):
    block = ref[:, 0]
    return block.reshape(block.shape[0] * block.shape[1], block.shape[2])


def joined_cols(ref):
    sides = [ref[:, c].reshape(-1, ref.shape[3]) for c in range(ref.shape[1])]
    return jnp.concatenate(sides, axis=1)


def prep(raw, gain, cosine, sine):
    normed = raw * inverse_rms(raw) * gain
    first, second = normed[:, : HD // 2], normed[:, HD // 2 :]
    return jnp.concatenate(
        [first * cosine - second * sine, second * cosine + first * sine], axis=1
    ).astype(BF16)


def prep_back(raw, gain, cosine, sine, grad):
    first, second = grad[:, : HD // 2], grad[:, HD // 2 :]
    turned = jnp.concatenate(
        [first * cosine + second * sine, second * cosine - first * sine], axis=1
    )
    inv = inverse_rms(raw)
    return norm_back(raw, inv, gain, turned).astype(BF16), gain_back(raw, inv, turned)


def attention_kernel(
    x_ref, wq_ref, wk_ref, wv_ref, wo_ref, g_in, g_attn, g_query, g_key, cos_ref, sin_ref, seg_col, seg_row,
    qraw_ref, kraw_ref, qh_ref, kh_ref, v_ref, attn_ref, yo_ref, middle_ref, a1_s,
):
    head = pl.program_id(1)
    cosine, sine = cos_ref[...], sin_ref[...]

    @pl.when(head == 0)
    def _():
        x = x_ref[...].astype(F32)
        a1 = (x * inverse_rms(x) * g_in[...]).astype(BF16)
        a1_s[...] = a1
        k_raw = dot(a1, joined_cols(wk_ref))
        kraw_ref[...] = k_raw
        kh_ref[...] = prep(k_raw, g_key[...], cosine, sine)
        v_ref[...] = dot(a1, joined_cols(wv_ref)).astype(BF16)
        yo_ref[...] = jnp.zeros_like(yo_ref)

    q_raw = dot(a1_s[...], joined(wq_ref))
    qraw_ref[...] = q_raw
    qh_ref[...] = prep(q_raw, g_query[...], cosine, sine)
    for start in range(0, LEN, BLOCK):
        low, high = window(start)
        rows = slice(start, high)
        scores = dot_cols(qh_ref[rows, :] * SCALE, kh_ref[low:high, :])
        place_q = start + lax.broadcasted_iota(jnp.int32, scores.shape, 0)
        place_k = low + lax.broadcasted_iota(jnp.int32, scores.shape, 1)
        allowed = (place_q >= place_k) & (seg_col[rows, :] == seg_row[0][:, low:high])
        scores = jnp.where(allowed, scores, MASK_VALUE)
        exps = jnp.exp(scores - jnp.max(scores, axis=1, keepdims=True))
        probs = (exps * (1.0 / jnp.sum(exps, axis=1, keepdims=True))).astype(BF16)
        attn_ref[rows, :] = dot(probs, v_ref[low:high, :]).astype(BF16)
    yo_ref[...] += dot_cols(attn_ref[...], joined(wo_ref))

    @pl.when(head == HEADS - 1)
    def _():
        y_o = yo_ref[...]
        middle_ref[...] = x_ref[...].astype(F32) + y_o * inverse_rms(y_o) * g_attn[...]


def attention_back_kernel(
    x_ref, wq_ref, wk_ref, wv_ref, wo_ref, g_in, g_attn, g_query, g_key, cos_ref, sin_ref, seg_col, seg_row,
    qraw_ref, kraw_ref, qh_ref, kh_ref, v_ref, attn_ref, yo_ref, dmid_ref,
    gw_q, gw_k, gw_v, gw_o, gx_ref, gg_in, gg_attn, gg_query, gg_key,
    a1_s, dyo_s, dq_s, dk_s, dv_s, da1_s, g_s,
):
    head = pl.program_id(1)
    cosine, sine = cos_ref[...], sin_ref[...]

    @pl.when(head == 0)
    def _():
        x = x_ref[...].astype(F32)
        a1_s[...] = (x * inverse_rms(x) * g_in[...]).astype(BF16)
        y_o, d_middle = yo_ref[...], dmid_ref[...]
        inv = inverse_rms(y_o)
        dyo_s[...] = norm_back(y_o, inv, g_attn[...], d_middle).astype(BF16)
        gg_attn[...] = gain_back(y_o, inv, d_middle)[None]
        dk_s[...] = jnp.zeros_like(dk_s)
        dv_s[...] = jnp.zeros_like(dv_s)
        da1_s[...] = jnp.zeros_like(da1_s)
        gg_query[...] = jnp.zeros_like(gg_query)

    d_yo, a1 = dyo_s[...], a1_s[...]
    gw_o[...] = dot_rows(d_yo, attn_ref[...]).astype(BF16).reshape(gw_o.shape)
    g_s[...] = dot(d_yo, joined(wo_ref)).astype(BF16)
    for start in range(0, LEN, BLOCK):
        low, high = window(start)
        rows = slice(start, high)
        query, grad = qh_ref[rows, :] * SCALE, g_s[rows, :]
        scores = dot_cols(kh_ref[low:high, :], query)
        place_k = low + lax.broadcasted_iota(jnp.int32, scores.shape, 0)
        place_q = start + lax.broadcasted_iota(jnp.int32, scores.shape, 1)
        allowed = (place_q >= place_k) & (seg_col[low:high, :] == seg_row[0][:, rows])
        scores = jnp.where(allowed, scores, MASK_VALUE)
        exps = jnp.exp(scores - jnp.max(scores, axis=0, keepdims=True))
        probs = exps * (1.0 / jnp.sum(exps, axis=0, keepdims=True))
        dp = dot_cols(v_ref[low:high, :], grad)
        ds = (probs * (dp - jnp.sum(dp * probs, axis=0, keepdims=True))).astype(BF16)
        dq_s[rows, :] = dot_rows(ds, kh_ref[low:high, :]) * SCALE
        dk_s[low:high, :] += dot(ds, query)
        dv_s[low:high, :] += dot(probs.astype(BF16), grad)
    d_q, gg = prep_back(qraw_ref[...], g_query[...], cosine, sine, dq_s[...])
    gg_query[...] += gg[None]
    gw_q[...] = dot_rows(a1, d_q).astype(BF16).reshape(gw_q.shape)
    da1_s[...] += dot_cols(d_q, joined(wq_ref))

    @pl.when(head == HEADS - 1)
    def _():
        d_k, gg = prep_back(kraw_ref[...], g_key[...], cosine, sine, dk_s[...])
        gg_key[...] = gg[None]
        d_v = dv_s[...].astype(BF16)
        for ref, grad in ((gw_k, d_k), (gw_v, d_v)):
            whole = dot_rows(a1, grad).astype(BF16)
            width = ref.shape[3]
            for c in range(ref.shape[1]):
                ref[:, c] = whole[:, c * width : (c + 1) * width].reshape(ref.shape[0], ref.shape[2], width)
        d_a1 = da1_s[...] + dot_cols(d_k, joined_cols(wk_ref)) + dot_cols(d_v, joined_cols(wv_ref))
        x = x_ref[...].astype(F32)
        inv = inverse_rms(x)
        gx_ref[...] = (dmid_ref[...] + norm_back(x, inv, g_in[...], d_a1)).astype(BF16)
        gg_in[...] = gain_back(x, inv, d_a1)[None]


def attention_specs(weights):
    rows, cols, depth, width = weights.shape
    per = HEADS // cols
    narrow = HD // cols
    wide = per * HD

    def token(width):
        return pl.BlockSpec((LEN, width), lambda s, h: (s, 0))

    def fixed(width):
        return pl.BlockSpec((1, width), lambda s, h: (0, 0))

    def heads(first):
        return pl.BlockSpec((rows, 1, depth, HD), lambda s, h: (0, h // per, 0, first + h % per))

    def share(which):
        return pl.BlockSpec((rows, cols, depth, narrow), lambda s, h: (0, 0, 0, which))

    base = wide // narrow
    in_specs = [
        token(D), heads(0), share(base), share(base + 1), heads((wide + 2 * narrow) // HD),
        fixed(D), fixed(D), fixed(HD), fixed(HD), token(HD // 2), token(HD // 2),
        token(1), pl.BlockSpec((1, 1, LEN), lambda s, h: (s, 0, 0)),
    ]
    head = pl.BlockSpec((LEN, HD), lambda s, h: (s, h))
    saved = [head, token(HD), head, token(HD), token(HD), head, token(D)]
    return in_specs, saved, token(D), heads, share, fixed


def attention_inputs(x, weights, gains, cosine, sine, segs):
    return (x, weights, weights, weights, weights, *[g[None] for g in gains], cosine, sine, segs[:, None], segs.reshape(-1, 1, LEN))


def attention(inputs):
    x, weights = inputs[:2]
    count = x.shape[0]
    in_specs, saved, token = attention_specs(weights)[:3]
    wide = HEADS * HD
    shapes = [(wide, F32), (HD, F32), (wide, BF16), (HD, BF16), (HD, BF16), (wide, BF16), (D, F32), (D, F32)]
    return pl.pallas_call(
        attention_kernel,
        grid=(count // LEN, HEADS),
        in_specs=in_specs,
        out_specs=[*saved, token],
        out_shape=[jax.ShapeDtypeStruct((count, width), kind) for width, kind in shapes],
        scratch_shapes=[pltpu.VMEM((LEN, D), BF16)],
        compiler_params=pltpu.CompilerParams(vmem_limit_bytes=60 << 20),
        cost_estimate=pl.CostEstimate(flops=count * (4 * D * 1280 + 4096 * 576), bytes_accessed=count * 16384, transcendentals=count * 2304),
    )(*inputs)


def attention_back(inputs, saved, d_middle):
    x, weights = inputs[:2]
    count = x.shape[0]
    rows, cols, depth, _ = weights.shape
    in_specs, saved_specs, token, heads, share, fixed = attention_specs(weights)
    wide_grad = jax.ShapeDtypeStruct((rows, cols, depth, HEADS // cols * HD), BF16)
    narrow_grad = jax.ShapeDtypeStruct((rows, cols, depth, HD // cols), BF16)
    gains = [D, D, HD, HD]
    return pl.pallas_call(
        attention_back_kernel,
        grid=(count // LEN, HEADS),
        in_specs=[*in_specs, *saved_specs, token],
        out_specs=[heads(0), share(0), share(0), heads(0), token, *[fixed(g) for g in gains]],
        out_shape=[
            wide_grad, narrow_grad, narrow_grad, wide_grad,
            jax.ShapeDtypeStruct((count, D), BF16),
            *[jax.ShapeDtypeStruct((1, g), F32) for g in gains],
        ],
        scratch_shapes=[
            pltpu.VMEM((LEN, D), BF16),
            pltpu.VMEM((LEN, D), BF16),
            pltpu.VMEM((LEN, HD), F32),
            pltpu.VMEM((LEN, HD), F32),
            pltpu.VMEM((LEN, HD), F32),
            pltpu.VMEM((LEN, D), F32),
            pltpu.VMEM((LEN, HD), BF16),
        ],
        compiler_params=pltpu.CompilerParams(vmem_limit_bytes=60 << 20),
        cost_estimate=pl.CostEstimate(flops=count * (8 * D * 1280 + 10240 * 576), bytes_accessed=count * 20000, transcendentals=count * 2304),
    )(*inputs, *saved, d_middle)


CHUNK = 512


def ffn_kernel(
    middle_ref, e0_ref, wg_ref, wu_ref, wd_ref, g_pre, g_ffn,
    out_ref, d_middle_ref, gg_ffn_ref, gg_pre_ref, gw_gate, gw_up, gw_down,
    a2_s, gate_s, up_s, hidden_s, yf_s, dyf_s,
):
    second, chunk = pl.program_id(0) == 1, pl.program_id(1)
    last = chunk == pl.num_programs(1) - 1

    @pl.when(jnp.logical_not(second) & (chunk == 0))
    def _():
        middle = middle_ref[...]
        a2_s[...] = (middle * inverse_rms(middle) * g_pre[...]).astype(BF16)
        yf_s[...] = jnp.zeros_like(yf_s)

    @pl.when(jnp.logical_not(second))
    def _():
        a2 = a2_s[...]
        gate = dot(a2, joined(wg_ref))
        up = dot(a2, joined(wu_ref))
        gate_s[chunk] = gate
        up_s[chunk] = up
        hidden = (jax.nn.gelu(gate, approximate=True) * up).astype(BF16)
        hidden_s[chunk] = hidden
        yf_s[...] += dot_cols(hidden, joined(wd_ref))

    @pl.when(jnp.logical_not(second) & last)
    def _():
        y_f, e0 = yf_s[...], e0_ref[...].astype(F32)
        inv = inverse_rms(y_f)
        out_ref[...] = (middle_ref[...] + y_f * inv * g_ffn[...]).astype(BF16)
        dyf_s[...] = norm_back(y_f, inv, g_ffn[...], e0).astype(BF16)
        gg_ffn_ref[...] = gain_back(y_f, inv, e0)[None]
        yf_s[...] = jnp.zeros_like(yf_s)

    @pl.when(second)
    def _():
        d_yf, a2 = dyf_s[...], a2_s[...]
        gate, up = gate_s[chunk], up_s[chunk]
        d_hidden = dot(d_yf, joined(wd_ref))
        square = gate * gate
        inner = GELU_C * gate * (1.0 + 0.044715 * square)
        tanh = jnp.tanh(inner)
        half = 0.5 * (1.0 + tanh)
        slope = half + 0.5 * gate * (1.0 - tanh * tanh) * (GELU_C * (1.0 + 0.134145 * square))
        d_gate = (d_hidden * up * slope).astype(BF16)
        d_up = (d_hidden * (gate * half)).astype(BF16)
        gw_gate[...] = dot_rows(a2, d_gate).astype(BF16).reshape(gw_gate.shape)
        gw_up[...] = dot_rows(a2, d_up).astype(BF16).reshape(gw_up.shape)
        gw_down[...] = dot_rows(d_yf, hidden_s[chunk]).astype(BF16).reshape(gw_down.shape)
        yf_s[...] += dot_cols(d_gate, joined(wg_ref)) + dot_cols(d_up, joined(wu_ref))

    @pl.when(second & last)
    def _():
        middle, d_a2 = middle_ref[...], yf_s[...]
        inv = inverse_rms(middle)
        d_middle_ref[...] = e0_ref[...].astype(F32) + norm_back(middle, inv, g_pre[...], d_a2)
        gg_pre_ref[...] = gain_back(middle, inv, d_a2)[None]


GELU_C = math.sqrt(2.0 / math.pi)


def ffn(middle, e0, weights, g_pre, g_ffn):
    count = middle.shape[0]
    rows, cols, depth = weights.shape[:3]
    width = weights.shape[3] // 3
    per = width // CHUNK
    chunks = cols * per
    once = pl.Buffered(1)

    def weight(which):
        return pl.BlockSpec((rows, 1, depth, CHUNK), lambda p, t: (0, t // per, 0, which * per + t % per))

    def whole(shape):
        return pl.BlockSpec(shape, lambda p, t: (0, 0), pipeline_mode=once)

    grad = pl.BlockSpec((rows, 1, depth, CHUNK), lambda p, t: (0, (p * t) // per, 0, (p * t) % per))
    grad_shape = jax.ShapeDtypeStruct((rows, cols, depth, width), BF16)
    return pl.pallas_call(
        ffn_kernel,
        grid=(2, chunks),
        in_specs=[whole((count, D)), whole((count, D)), weight(0), weight(1), weight(2), whole((1, D)), whole((1, D))],
        out_specs=[whole((count, D)), whole((count, D)), whole((1, D)), whole((1, D)), grad, grad, grad],
        out_shape=[
            jax.ShapeDtypeStruct((count, D), BF16),
            jax.ShapeDtypeStruct((count, D), F32),
            jax.ShapeDtypeStruct((1, D), F32),
            jax.ShapeDtypeStruct((1, D), F32),
            grad_shape, grad_shape, grad_shape,
        ],
        scratch_shapes=[
            pltpu.VMEM((count, D), BF16),
            pltpu.VMEM((chunks, count, CHUNK), F32),
            pltpu.VMEM((chunks, count, CHUNK), F32),
            pltpu.VMEM((chunks, count, CHUNK), BF16),
            pltpu.VMEM((count, D), F32),
            pltpu.VMEM((count, D), BF16),
        ],
        compiler_params=pltpu.CompilerParams(vmem_limit_bytes=60 << 20),
        cost_estimate=pl.CostEstimate(flops=18 * count * D * FF, bytes_accessed=36 * D * FF, transcendentals=2 * count * FF),
    )(middle, e0, weights, weights, weights, g_pre[None], g_ffn[None])


def local(
    tokens,
    w_query,
    w_key,
    w_value,
    w_out,
    w_gate,
    w_up,
    w_down,
    gain_input,
    gain_post_attn,
    gain_pre_ffn,
    gain_post_ffn,
    gain_query,
    gain_key,
    segment_ids,
    positions,
    cotangent,
):
    rows, cols = lax.axis_size("row"), lax.axis_size("col")
    place = lax.axis_index("row") * cols + lax.axis_index("col")
    count = tokens.shape[0] // (rows * cols)
    assert count == LEN
    width = gain_input.shape[0]
    wide, narrow, ff_width = w_query.shape[1], w_key.shape[1], w_gate.shape[1]

    gains = lax.all_gather(
        jnp.stack([gain_input, gain_post_attn, gain_pre_ffn, gain_post_ffn]), GROUP, axis=1, tiled=True
    )
    attn_w = gather_blocks(jnp.concatenate([w_query, w_key, w_value, w_out.T], axis=1))
    x = to_tokens(tokens)
    ffn_w = gather_blocks(jnp.concatenate([w_gate, w_up, w_down.T], axis=1))
    e0 = to_tokens(cotangent)
    segs = lax.dynamic_slice_in_dim(segment_ids, place * count, count)
    cosine, sine = rotary_tables(lax.dynamic_slice_in_dim(positions, place * count, count))

    inputs = attention_inputs(
        x, attn_w, (gains[0], gains[1], gain_query, gain_key), cosine, sine, segs
    )
    *saved, middle = attention(inputs)
    result, d_middle, gg_ffn, gg_pre, gw_gate, gw_up, gw_down = ffn(
        middle, e0, ffn_w, gains[2], gains[3]
    )
    ffn_own = scatter_blocks(jnp.concatenate([gw_gate, gw_up, gw_down], axis=3))
    output = to_features(result)
    gw_q, gw_k, gw_v, gw_o, grad_x, gg_in, gg_attn, gg_query, gg_key = attention_back(
        inputs, saved, d_middle
    )
    gw_attn, ffn_own = lax.optimization_barrier(
        (jnp.concatenate([gw_q, gw_k, gw_v, gw_o], axis=3), ffn_own)
    )
    attn_own = scatter_blocks(gw_attn)
    ffn_grads = lax.psum(ffn_own, "dp")
    ffn_grads, attn_own = lax.optimization_barrier((ffn_grads, attn_own))
    ffn_grads = ffn_grads.astype(F32)
    attn_grads = lax.psum(attn_own, "dp").astype(F32)
    grad_tokens = to_features(grad_x)

    sums = lax.psum(
        jnp.concatenate([gg_in, gg_attn, gg_pre, gg_ffn, gg_query, gg_key], axis=1)[0],
        ("dp", "row", "col"),
    )
    own = lax.dynamic_slice_in_dim(sums[: 4 * D].reshape(4, D), place * width, width, 1)
    return (
        output,
        grad_tokens,
        attn_grads[:, :wide],
        attn_grads[:, wide : wide + narrow],
        attn_grads[:, wide + narrow : wide + 2 * narrow],
        attn_grads[:, wide + 2 * narrow :].T,
        ffn_grads[:, :ff_width],
        ffn_grads[:, ff_width : 2 * ff_width],
        ffn_grads[:, 2 * ff_width :].T,
        own[0],
        own[1],
        own[2],
        own[3],
        sums[4 * D : 4 * D + HD],
        sums[4 * D + HD :],
    )


def solution(mesh):
    tokens, block, turned, gain = P("dp", GROUP), P("row", "col"), P("col", "row"), P(GROUP)
    in_specs = (
        tokens, block, block, block, turned, block, block, turned,
        gain, gain, gain, gain, P(), P(), P("dp"), P("dp"), tokens,
    )
    out_specs = (
        tokens, tokens, block, block, block, turned, block, block, turned,
        gain, gain, gain, gain, P(), P(),
    )
    return jax.shard_map(local, mesh=mesh, in_specs=in_specs, out_specs=out_specs, check_vma=False)
```

```python
import math

import jax
import jax.numpy as jnp
from jax import lax
from jax.experimental import pallas as pl
from jax.experimental.pallas import tpu as pltpu
from jax.sharding import PartitionSpec as P

D = 640
HEADS = 4
HD = 256
FF = 2048
LEN = 1024

EPSILON = 1e-06
ROPE_BASE = 1000000.0
MASK_VALUE = -1000000000.0
GROUP = ("row", "col")
BF16 = jnp.bfloat16
F32 = jnp.float32
SCALE = HD ** -0.5


def dot(left, right):
    return jnp.dot(left, right, preferred_element_type=F32)


def dot_rows(left, right):
    return lax.dot_general(left, right, (((0,), (0,)), ((), ())), preferred_element_type=F32)


def dot_cols(left, right):
    return lax.dot_general(left, right, (((1,), (1,)), ((), ())), preferred_element_type=F32)


def inverse_rms(values):
    return lax.rsqrt(jnp.mean(values * values, axis=-1, keepdims=True) + EPSILON)


def norm_back(values, inv_rms, gain, grad):
    weighted = grad * gain
    inner = jnp.mean(weighted * values, axis=-1, keepdims=True)
    return inv_rms * weighted - values * (inv_rms * inv_rms * inv_rms * inner)


def gain_back(values, inv_rms, grad):
    return jnp.sum(grad * values * inv_rms, axis=0)


def rotary_tables(positions):
    half = HD // 2
    frequency = jnp.exp(jnp.arange(half, dtype=F32) * (-2.0 * math.log(ROPE_BASE) / HD))
    angles = positions.astype(F32)[:, None] * frequency[None, :]
    return (jnp.cos(angles), jnp.sin(angles))


def gather_blocks(block):
    rows, cols = lax.axis_size("row"), lax.axis_size("col")
    return lax.all_gather(block, GROUP).reshape(rows, cols, *block.shape)


def col_first(grads):
    return jnp.concatenate([g.transpose(1, 0, 2, 3) for g in grads], axis=3)


def neighbours(axis, mask):
    return [(i, i ^ mask) for i in range(lax.axis_size(axis))]


def halve(value, axis, mask):
    size = value.shape[0] // 2
    bit = (lax.axis_index(axis) // mask) % 2
    sent = lax.dynamic_slice_in_dim(value, (1 - bit) * size, size, 0)
    kept = lax.dynamic_slice_in_dim(value, bit * size, size, 0)
    got = lax.ppermute(sent, axis, neighbours(axis, mask))
    return (kept.astype(F32) + got.astype(F32)).astype(BF16)


def double(value, axis, mask):
    bit = (lax.axis_index(axis) // mask) % 2
    got = lax.ppermute(value, axis, neighbours(axis, mask))
    return jnp.concatenate([jnp.where(bit == 0, value, got), jnp.where(bit == 0, got, value)], axis=0)


def scatter_blocks(blocks):
    return halve(halve(blocks, "col", 1)[0], "row", 1)[0]


def masks(axis):
    size = lax.axis_size(axis)
    return [1 << bit for bit in range(size.bit_length() - 1)]


def total_halving(value):
    for mask in masks("dp"):
        value = halve(value, "dp", mask)
    for mask in reversed(masks("dp")):
        value = double(value, "dp", mask)
    return value


def total_small(value):
    for axis in ("col", "row", "dp"):
        for mask in masks(axis):
            value = value + lax.ppermute(value, axis, neighbours(axis, mask))
    return value


def partners():
    rows, cols = lax.axis_size("row"), lax.axis_size("col")
    place = lax.axis_index("row") * cols + lax.axis_index("col")
    count = rows * cols
    swaps = [[(i, i ^ mask) for i in range(count)] for mask in range(count)]
    return place, count, swaps


def by_place(parts, place):
    stacked = jnp.stack(parts)
    return [lax.dynamic_index_in_dim(stacked, place ^ j, 0, keepdims=False) for j in range(len(parts))]


def swap(part, perm):
    return lax.ppermute(part, GROUP, perm)


def to_tokens(block):
    place, count, swaps = partners()
    size = block.shape[0] // count
    parts = [lax.dynamic_slice_in_dim(block, (place ^ m) * size, size, 0) for m in range(count)]
    parts = parts[:1] + [swap(parts[m], swaps[m]) for m in range(1, count)]
    return jnp.concatenate(by_place(parts, place), axis=1)


def to_features(block):
    place, count, swaps = partners()
    size = block.shape[1] // count
    parts = [lax.dynamic_slice_in_dim(block, (place ^ m) * size, size, 1) for m in range(count)]
    parts = parts[:1] + [swap(parts[m], swaps[m]) for m in range(1, count)]
    return jnp.concatenate(by_place(parts, place), axis=0)


BLOCK = 256
REACH = 512


def window(start):
    return max(0, start - REACH), start + BLOCK


def joined(ref):
    block = ref[:, 0]
    return block.reshape(block.shape[0] * block.shape[1], block.shape[2])


def joined_cols(ref):
    sides = [ref[:, c].reshape(-1, ref.shape[3]) for c in range(ref.shape[1])]
    return jnp.concatenate(sides, axis=1)


def prep(raw, gain, cosine, sine):
    normed = raw * inverse_rms(raw) * gain
    first, second = normed[:, : HD // 2], normed[:, HD // 2 :]
    return jnp.concatenate(
        [first * cosine - second * sine, second * cosine + first * sine], axis=1
    ).astype(BF16)


def prep_back(raw, gain, cosine, sine, grad):
    first, second = grad[:, : HD // 2], grad[:, HD // 2 :]
    turned = jnp.concatenate(
        [first * cosine + second * sine, second * cosine - first * sine], axis=1
    )
    inv = inverse_rms(raw)
    return norm_back(raw, inv, gain, turned).astype(BF16), gain_back(raw, inv, turned)


def attention_kernel(
    x_ref, wq_ref, wk_ref, wv_ref, wo_ref, g_in, g_attn, g_query, g_key, cos_ref, sin_ref, seg_col, seg_row,
    qraw_ref, kraw_ref, qh_ref, kh_ref, v_ref, attn_ref, yo_ref, middle_ref, a1_s,
):
    head = pl.program_id(1)
    cosine, sine = cos_ref[...], sin_ref[...]

    @pl.when(head == 0)
    def _():
        x = x_ref[...].astype(F32)
        a1 = (x * inverse_rms(x) * g_in[...]).astype(BF16)
        a1_s[...] = a1
        k_raw = dot(a1, joined_cols(wk_ref))
        kraw_ref[...] = k_raw
        kh_ref[...] = prep(k_raw, g_key[...], cosine, sine)
        v_ref[...] = dot(a1, joined_cols(wv_ref)).astype(BF16)
        yo_ref[...] = jnp.zeros_like(yo_ref)

    q_raw = dot(a1_s[...], joined(wq_ref))
    qraw_ref[...] = q_raw
    qh_ref[...] = prep(q_raw, g_query[...], cosine, sine)
    for start in range(0, LEN, BLOCK):
        low, high = window(start)
        rows = slice(start, high)
        scores = dot_cols(qh_ref[rows, :] * SCALE, kh_ref[low:high, :])
        place_q = start + lax.broadcasted_iota(jnp.int32, scores.shape, 0)
        place_k = low + lax.broadcasted_iota(jnp.int32, scores.shape, 1)
        allowed = (place_q >= place_k) & (seg_col[rows, :] == seg_row[0][:, low:high])
        scores = jnp.where(allowed, scores, MASK_VALUE)
        exps = jnp.exp(scores - jnp.max(scores, axis=1, keepdims=True))
        probs = (exps * (1.0 / jnp.sum(exps, axis=1, keepdims=True))).astype(BF16)
        attn_ref[rows, :] = dot(probs, v_ref[low:high, :]).astype(BF16)
    yo_ref[...] += dot_cols(attn_ref[...], joined(wo_ref))

    @pl.when(head == HEADS - 1)
    def _():
        y_o = yo_ref[...]
        middle_ref[...] = x_ref[...].astype(F32) + y_o * inverse_rms(y_o) * g_attn[...]


def attention_back_kernel(
    x_ref, wq_ref, wk_ref, wv_ref, wo_ref, g_in, g_attn, g_query, g_key, cos_ref, sin_ref, seg_col, seg_row,
    qraw_ref, kraw_ref, qh_ref, kh_ref, v_ref, attn_ref, yo_ref, dmid_ref,
    gw_q, gw_k, gw_v, gw_o, gx_ref, gg_in, gg_attn, gg_query, gg_key,
    a1_s, dyo_s, dq_s, dk_s, dv_s, da1_s, g_s,
):
    head = pl.program_id(1)
    cosine, sine = cos_ref[...], sin_ref[...]

    @pl.when(head == 0)
    def _():
        x = x_ref[...].astype(F32)
        a1_s[...] = (x * inverse_rms(x) * g_in[...]).astype(BF16)
        y_o, d_middle = yo_ref[...], dmid_ref[...]
        inv = inverse_rms(y_o)
        dyo_s[...] = norm_back(y_o, inv, g_attn[...], d_middle).astype(BF16)
        gg_attn[...] = gain_back(y_o, inv, d_middle)[None]
        dk_s[...] = jnp.zeros_like(dk_s)
        dv_s[...] = jnp.zeros_like(dv_s)
        da1_s[...] = jnp.zeros_like(da1_s)
        gg_query[...] = jnp.zeros_like(gg_query)

    d_yo, a1 = dyo_s[...], a1_s[...]
    gw_o[...] = dot_rows(d_yo, attn_ref[...]).astype(BF16).reshape(gw_o.shape)
    g_s[...] = dot(d_yo, joined(wo_ref)).astype(BF16)
    for start in range(0, LEN, BLOCK):
        low, high = window(start)
        rows = slice(start, high)
        query, grad = qh_ref[rows, :] * SCALE, g_s[rows, :]
        scores = dot_cols(kh_ref[low:high, :], query)
        place_k = low + lax.broadcasted_iota(jnp.int32, scores.shape, 0)
        place_q = start + lax.broadcasted_iota(jnp.int32, scores.shape, 1)
        allowed = (place_q >= place_k) & (seg_col[low:high, :] == seg_row[0][:, rows])
        scores = jnp.where(allowed, scores, MASK_VALUE)
        exps = jnp.exp(scores - jnp.max(scores, axis=0, keepdims=True))
        probs = exps * (1.0 / jnp.sum(exps, axis=0, keepdims=True))
        dp = dot_cols(v_ref[low:high, :], grad)
        ds = (probs * (dp - jnp.sum(dp * probs, axis=0, keepdims=True))).astype(BF16)
        dq_s[rows, :] = dot_rows(ds, kh_ref[low:high, :]) * SCALE
        dk_s[low:high, :] += dot(ds, query)
        dv_s[low:high, :] += dot(probs.astype(BF16), grad)
    d_q, gg = prep_back(qraw_ref[...], g_query[...], cosine, sine, dq_s[...])
    gg_query[...] += gg[None]
    gw_q[...] = dot_rows(a1, d_q).astype(BF16).reshape(gw_q.shape)
    da1_s[...] += dot_cols(d_q, joined(wq_ref))

    @pl.when(head == HEADS - 1)
    def _():
        d_k, gg = prep_back(kraw_ref[...], g_key[...], cosine, sine, dk_s[...])
        gg_key[...] = gg[None]
        d_v = dv_s[...].astype(BF16)
        for ref, grad in ((gw_k, d_k), (gw_v, d_v)):
            whole = dot_rows(a1, grad).astype(BF16)
            width = ref.shape[3]
            for c in range(ref.shape[1]):
                ref[:, c] = whole[:, c * width : (c + 1) * width].reshape(ref.shape[0], ref.shape[2], width)
        d_a1 = da1_s[...] + dot_cols(d_k, joined_cols(wk_ref)) + dot_cols(d_v, joined_cols(wv_ref))
        x = x_ref[...].astype(F32)
        inv = inverse_rms(x)
        gx_ref[...] = (dmid_ref[...] + norm_back(x, inv, g_in[...], d_a1)).astype(BF16)
        gg_in[...] = gain_back(x, inv, d_a1)[None]


def attention_specs(weights):
    rows, cols, depth, width = weights.shape
    per = HEADS // cols
    narrow = HD // cols
    wide = per * HD

    def token(width):
        return pl.BlockSpec((LEN, width), lambda s, h: (s, 0))

    def fixed(width):
        return pl.BlockSpec((1, width), lambda s, h: (0, 0))

    def heads(first):
        return pl.BlockSpec((rows, 1, depth, HD), lambda s, h: (0, h // per, 0, first + h % per))

    def share(which):
        return pl.BlockSpec((rows, cols, depth, narrow), lambda s, h: (0, 0, 0, which))

    base = wide // narrow
    in_specs = [
        token(D), heads(0), share(base), share(base + 1), heads((wide + 2 * narrow) // HD),
        fixed(D), fixed(D), fixed(HD), fixed(HD), token(HD // 2), token(HD // 2),
        token(1), pl.BlockSpec((1, 1, LEN), lambda s, h: (s, 0, 0)),
    ]
    head = pl.BlockSpec((LEN, HD), lambda s, h: (s, h))
    saved = [head, token(HD), head, token(HD), token(HD), head, token(D)]
    return in_specs, saved, token(D), heads, share, fixed


def attention_inputs(x, weights, gains, cosine, sine, segs):
    return (x, weights, weights, weights, weights, *[g[None] for g in gains], cosine, sine, segs[:, None], segs.reshape(-1, 1, LEN))


def attention(inputs):
    x, weights = inputs[:2]
    count = x.shape[0]
    in_specs, saved, token = attention_specs(weights)[:3]
    wide = HEADS * HD
    shapes = [(wide, F32), (HD, F32), (wide, BF16), (HD, BF16), (HD, BF16), (wide, BF16), (D, F32), (D, F32)]
    return pl.pallas_call(
        attention_kernel,
        grid=(count // LEN, HEADS),
        in_specs=in_specs,
        out_specs=[*saved, token],
        out_shape=[jax.ShapeDtypeStruct((count, width), kind) for width, kind in shapes],
        scratch_shapes=[pltpu.VMEM((LEN, D), BF16)],
        compiler_params=pltpu.CompilerParams(vmem_limit_bytes=60 << 20),
        cost_estimate=pl.CostEstimate(flops=count * (4 * D * 1280 + 4096 * 576), bytes_accessed=count * 16384, transcendentals=count * 2304),
    )(*inputs)


def attention_back(inputs, saved, d_middle):
    x, weights = inputs[:2]
    count = x.shape[0]
    rows, cols, depth, _ = weights.shape
    in_specs, saved_specs, token, heads, share, fixed = attention_specs(weights)
    wide_grad = jax.ShapeDtypeStruct((rows, cols, depth, HEADS // cols * HD), BF16)
    narrow_grad = jax.ShapeDtypeStruct((rows, cols, depth, HD // cols), BF16)
    gains = [D, D, HD, HD]
    return pl.pallas_call(
        attention_back_kernel,
        grid=(count // LEN, HEADS),
        in_specs=[*in_specs, *saved_specs, token],
        out_specs=[heads(0), share(0), share(0), heads(0), token, *[fixed(g) for g in gains]],
        out_shape=[
            wide_grad, narrow_grad, narrow_grad, wide_grad,
            jax.ShapeDtypeStruct((count, D), BF16),
            *[jax.ShapeDtypeStruct((1, g), F32) for g in gains],
        ],
        scratch_shapes=[
            pltpu.VMEM((LEN, D), BF16),
            pltpu.VMEM((LEN, D), BF16),
            pltpu.VMEM((LEN, HD), F32),
            pltpu.VMEM((LEN, HD), F32),
            pltpu.VMEM((LEN, HD), F32),
            pltpu.VMEM((LEN, D), F32),
            pltpu.VMEM((LEN, HD), BF16),
        ],
        compiler_params=pltpu.CompilerParams(vmem_limit_bytes=60 << 20),
        cost_estimate=pl.CostEstimate(flops=count * (8 * D * 1280 + 10240 * 576), bytes_accessed=count * 20000, transcendentals=count * 2304),
    )(*inputs, *saved, d_middle)


CHUNK = 512


def ffn_kernel(
    middle_ref, e0_ref, wg_ref, wu_ref, wd_ref, g_pre, g_ffn,
    out_ref, d_middle_ref, gg_ffn_ref, gg_pre_ref, gw_gate, gw_up, gw_down,
    a2_s, gate_s, up_s, hidden_s, yf_s, dyf_s,
):
    second, chunk = pl.program_id(0) == 1, pl.program_id(1)
    last = chunk == pl.num_programs(1) - 1

    @pl.when(jnp.logical_not(second) & (chunk == 0))
    def _():
        middle = middle_ref[...]
        a2_s[...] = (middle * inverse_rms(middle) * g_pre[...]).astype(BF16)
        yf_s[...] = jnp.zeros_like(yf_s)

    @pl.when(jnp.logical_not(second))
    def _():
        a2 = a2_s[...]
        gate = dot(a2, joined(wg_ref))
        up = dot(a2, joined(wu_ref))
        gate_s[chunk] = gate
        up_s[chunk] = up
        hidden = (jax.nn.gelu(gate, approximate=True) * up).astype(BF16)
        hidden_s[chunk] = hidden
        yf_s[...] += dot_cols(hidden, joined(wd_ref))

    @pl.when(jnp.logical_not(second) & last)
    def _():
        y_f, e0 = yf_s[...], e0_ref[...].astype(F32)
        inv = inverse_rms(y_f)
        out_ref[...] = (middle_ref[...] + y_f * inv * g_ffn[...]).astype(BF16)
        dyf_s[...] = norm_back(y_f, inv, g_ffn[...], e0).astype(BF16)
        gg_ffn_ref[...] = gain_back(y_f, inv, e0)[None]
        yf_s[...] = jnp.zeros_like(yf_s)

    @pl.when(second)
    def _():
        d_yf, a2 = dyf_s[...], a2_s[...]
        gate, up = gate_s[chunk], up_s[chunk]
        d_hidden = dot(d_yf, joined(wd_ref))
        square = gate * gate
        inner = GELU_C * gate * (1.0 + 0.044715 * square)
        tanh = jnp.tanh(inner)
        half = 0.5 * (1.0 + tanh)
        slope = half + 0.5 * gate * (1.0 - tanh * tanh) * (GELU_C * (1.0 + 0.134145 * square))
        d_gate = (d_hidden * up * slope).astype(BF16)
        d_up = (d_hidden * (gate * half)).astype(BF16)
        gw_gate[...] = dot_rows(a2, d_gate).astype(BF16).reshape(gw_gate.shape)
        gw_up[...] = dot_rows(a2, d_up).astype(BF16).reshape(gw_up.shape)
        gw_down[...] = dot_rows(d_yf, hidden_s[chunk]).astype(BF16).reshape(gw_down.shape)
        yf_s[...] += dot_cols(d_gate, joined(wg_ref)) + dot_cols(d_up, joined(wu_ref))

    @pl.when(second & last)
    def _():
        middle, d_a2 = middle_ref[...], yf_s[...]
        inv = inverse_rms(middle)
        d_middle_ref[...] = e0_ref[...].astype(F32) + norm_back(middle, inv, g_pre[...], d_a2)
        gg_pre_ref[...] = gain_back(middle, inv, d_a2)[None]


GELU_C = math.sqrt(2.0 / math.pi)


def ffn(middle, e0, weights, g_pre, g_ffn):
    count = middle.shape[0]
    rows, cols, depth = weights.shape[:3]
    width = weights.shape[3] // 3
    per = width // CHUNK
    chunks = cols * per
    once = pl.Buffered(1)

    def weight(which):
        return pl.BlockSpec((rows, 1, depth, CHUNK), lambda p, t: (0, t // per, 0, which * per + t % per))

    def whole(shape):
        return pl.BlockSpec(shape, lambda p, t: (0, 0), pipeline_mode=once)

    grad = pl.BlockSpec((rows, 1, depth, CHUNK), lambda p, t: (0, (p * t) // per, 0, (p * t) % per))
    grad_shape = jax.ShapeDtypeStruct((rows, cols, depth, width), BF16)
    return pl.pallas_call(
        ffn_kernel,
        grid=(2, chunks),
        in_specs=[whole((count, D)), whole((count, D)), weight(0), weight(1), weight(2), whole((1, D)), whole((1, D))],
        out_specs=[whole((count, D)), whole((count, D)), whole((1, D)), whole((1, D)), grad, grad, grad],
        out_shape=[
            jax.ShapeDtypeStruct((count, D), BF16),
            jax.ShapeDtypeStruct((count, D), F32),
            jax.ShapeDtypeStruct((1, D), F32),
            jax.ShapeDtypeStruct((1, D), F32),
            grad_shape, grad_shape, grad_shape,
        ],
        scratch_shapes=[
            pltpu.VMEM((count, D), BF16),
            pltpu.VMEM((chunks, count, CHUNK), F32),
            pltpu.VMEM((chunks, count, CHUNK), F32),
            pltpu.VMEM((chunks, count, CHUNK), BF16),
            pltpu.VMEM((count, D), F32),
            pltpu.VMEM((count, D), BF16),
        ],
        compiler_params=pltpu.CompilerParams(vmem_limit_bytes=60 << 20),
        cost_estimate=pl.CostEstimate(flops=18 * count * D * FF, bytes_accessed=36 * D * FF, transcendentals=2 * count * FF),
    )(middle, e0, weights, weights, weights, g_pre[None], g_ffn[None])


def local(
    tokens,
    w_query,
    w_key,
    w_value,
    w_out,
    w_gate,
    w_up,
    w_down,
    gain_input,
    gain_post_attn,
    gain_pre_ffn,
    gain_post_ffn,
    gain_query,
    gain_key,
    segment_ids,
    positions,
    cotangent,
):
    rows, cols = lax.axis_size("row"), lax.axis_size("col")
    place = lax.axis_index("row") * cols + lax.axis_index("col")
    count = tokens.shape[0] // (rows * cols)
    assert count == LEN
    width = gain_input.shape[0]
    wide, narrow, ff_width = w_query.shape[1], w_key.shape[1], w_gate.shape[1]

    gains = lax.all_gather(
        jnp.stack([gain_input, gain_post_attn, gain_pre_ffn, gain_post_ffn]), GROUP, axis=1, tiled=True
    )
    attn_w = gather_blocks(jnp.concatenate([w_query, w_key, w_value, w_out.T], axis=1))
    x = to_tokens(tokens)
    ffn_w = gather_blocks(jnp.concatenate([w_gate, w_up, w_down.T], axis=1))
    e0 = to_tokens(cotangent)
    segs = lax.dynamic_slice_in_dim(segment_ids, place * count, count)
    cosine, sine = rotary_tables(lax.dynamic_slice_in_dim(positions, place * count, count))

    inputs = attention_inputs(
        x, attn_w, (gains[0], gains[1], gain_query, gain_key), cosine, sine, segs
    )
    *saved, middle = attention(inputs)
    result, d_middle, gg_ffn, gg_pre, gw_gate, gw_up, gw_down = ffn(
        middle, e0, ffn_w, gains[2], gains[3]
    )
    ffn_own = scatter_blocks(col_first([gw_gate, gw_up, gw_down]))
    output = to_features(result)
    gw_q, gw_k, gw_v, gw_o, grad_x, gg_in, gg_attn, gg_query, gg_key = attention_back(
        inputs, saved, d_middle
    )
    attn_grads = total_halving(
        scatter_blocks(col_first([gw_q, gw_k, gw_v, gw_o]))
    ).astype(F32)
    ffn_grads = lax.psum(ffn_own, "dp").astype(F32)
    grad_tokens = to_features(grad_x)

    sums = total_small(
        jnp.concatenate([gg_in, gg_attn, gg_pre, gg_ffn, gg_query, gg_key], axis=1)[0]
    )
    own = lax.dynamic_slice_in_dim(sums[: 4 * D].reshape(4, D), place * width, width, 1)
    return (
        output,
        grad_tokens,
        attn_grads[:, :wide],
        attn_grads[:, wide : wide + narrow],
        attn_grads[:, wide + narrow : wide + 2 * narrow],
        attn_grads[:, wide + 2 * narrow :].T,
        ffn_grads[:, :ff_width],
        ffn_grads[:, ff_width : 2 * ff_width],
        ffn_grads[:, 2 * ff_width :].T,
        own[0],
        own[1],
        own[2],
        own[3],
        sums[4 * D : 4 * D + HD],
        sums[4 * D + HD :],
    )


def solution(mesh):
    tokens, block, turned, gain = P("dp", GROUP), P("row", "col"), P("col", "row"), P(GROUP)
    in_specs = (
        tokens, block, block, block, turned, block, block, turned,
        gain, gain, gain, gain, P(), P(), P("dp"), P("dp"), tokens,
    )
    out_specs = (
        tokens, tokens, block, block, block, turned, block, block, turned,
        gain, gain, gain, gain, P(), P(),
    )
    return jax.shard_map(local, mesh=mesh, in_specs=in_specs, out_specs=out_specs, check_vma=False)
```
